512 devices in a mesh: row: 32 (over y, z_lo), col: 16 (over x, z_hi, core).
Axes of the slice: x: 4, y: 8, z: 8 (z_hi: 2, z_lo: 4; z = z_hi * 4 + z_lo), core: 2. Of those that a mesh axis runs over, the one named last changes fastest.
Arguments:
- b_old: float32 [65536, 128], P('col'), may hold values from 0.2 to 2
- positions: float32 [3, 65536], P(None, 'col'), may hold values from -1 to 1
- angles: float32 [2, 65536], P(None, 'col'), may hold values from -3.140625 to 3.140625
- areas: float32 [65536], P('col'), may hold values from 0.00030517578 to 0.0045776367
- visible: int32 [128, 128], replicated, may hold values from 0 to 1
- assign: int32 [65536], P('col'), may hold values from 0 to 127, never falling along the last dimension, each value on 1 to 1024 neighbouring positions
- emission: float32 [65536, 128], P(('row', 'col')), may hold values from 0 to 1
- reflect: float32 [65536, 128], P(('row', 'col')), may hold values from 0.2 to 0.95
Outputs:
- b_new: float32 [65536, 128], P(('row', 'col'))
The draws below stay inside these ranges and needn't reach their ends.
Inputs may be any that keep to these rules, and one draw needn't show every extreme that they name: assign never falls along the facets; every block holds 1 to 1024 facets.
All inputs are finite; a program needn't handle non-finite values.
Results may differ from the reference program's by a relative error of at most 0.0003.
Values sent between devices are 32-bit elements; how exact they have to be, the bound alone decides.
A program may use at most 64 MiB of HBM per device.

```python
import math
import jax
import jax.numpy as jnp
import numpy as np
from jax import lax

BANDS = 128
FACETS = 65536
BLOCKS = 128
BLOCK_MOST = 1024


def draw_visible(key, part):
    key = jax.random.fold_in(key, 11)
    key_level, key_roll = jax.random.split(key)
    level = jax.random.randint(key_level, (BLOCKS,), 0, 7)
    threshold = jnp.left_shift(jnp.ones((BLOCKS,), jnp.int32), level)
    rolled = jax.random.randint(key_roll, (BLOCKS, BLOCKS), 0, 64)
    return (rolled < threshold[None, :]).astype(jnp.int32)


def level_of(rng, shape, cuts, least, high):
    gain = 1.0
    for dim, parts in cuts:
        steps = jax.random.uniform(jax.random.fold_in(jax.random.fold_in(rng, 6), dim), (parts,), jnp.float32, least / len(cuts), high / len(cuts))
        gain = gain * jnp.repeat(jnp.exp(steps), shape[dim] // parts).reshape((-1,) + (1,) * (len(shape) - 1 - dim))
    return gain


def length_profile(amount, total, most, skew):
    portions = [(1 << 20) // math.isqrt(rank ** skew) + 1 for rank in range(2, amount + 1)]
    surplus, counts = total - most - (amount - 1), [1] * (amount - 1)
    while surplus > 0:
        movable = [i for i in range(amount - 1) if counts[i] < most]
        whole, left = sum([portions[i] for i in movable]), surplus
        for i in movable:
            addition = min(most - counts[i], max(1, left * portions[i] // whole), surplus)
            counts[i] = counts[i] + addition
            surplus = surplus - addition
    return np.array([most] + counts)


def uneven(own_key, number_of, total, reach, slope):
    if number_of == 2:
        one = jax.random.randint(own_key, (), max(1, total - reach), min(reach, total - 1) + 1)
        return jnp.stack([one, total - one])
    sizes = jnp.asarray(length_profile(number_of, total, reach, slope), jnp.int32)
    couples = (number_of - 1) // 2
    giver, sink = sizes[1:1 + 2 * couples:2], sizes[2:2 + 2 * couples:2]
    slack = jnp.minimum(giver - 1, reach - sink)
    passed = jax.random.randint(jax.random.fold_in(own_key, 1), (couples,), 0, 1 << 20) % (slack + 1)
    sizes = sizes.at[1:1 + 2 * couples:2].set(giver - passed).at[2:2 + 2 * couples:2].set(sink + passed)
    return sizes[jax.random.permutation(jax.random.fold_in(own_key, 2), number_of)]


def setup_inputs(seed: int = 0) -> dict:
    streams_of = jax.random.split(jax.random.key(seed), 9)
    return {
        "b_old": jnp.clip(jnp.exp(math.log(2.0) - 2.3025851 * jax.random.uniform(streams_of[0], (FACETS, BANDS), jnp.float32) ** level_of(streams_of[0], (FACETS, BANDS), ((0, 16),), -0.2, 0.2)), 0.2, 2.0),
        "positions": jnp.clip(jax.random.uniform(streams_of[1], (3, FACETS), jnp.float32, -1.0, 1.0) * level_of(streams_of[1], (3, FACETS), ((1, 16),), -0.4, 0.0), -1.0, 1.0),
        "angles": jnp.clip(jax.random.uniform(streams_of[2], (2, FACETS), jnp.float32, -3.140625, 3.140625), -3.140625, 3.140625),
        "areas": jnp.clip(jnp.exp(math.log(0.0045776367) - 2.7080502 * jax.random.uniform(streams_of[3], (FACETS,), jnp.float32) ** level_of(streams_of[3], (FACETS,), ((0, 16),), -0.2, 0.2)), 0.00030517578, 0.0045776367),
        "visible": draw_visible(jax.random.fold_in(streams_of[8], 71), 0),
        "assign": jnp.searchsorted(jnp.cumsum(uneven(streams_of[5], BLOCKS, FACETS, BLOCK_MOST, 1)), jnp.arange(FACETS), side="right").astype(jnp.int32),
        "emission": jnp.clip(1.0 * jax.random.uniform(streams_of[6], (FACETS, BANDS), jnp.float32) ** level_of(streams_of[6], (FACETS, BANDS), ((0, 512),), -0.2, 0.2), 0.0, 1.0),
        "reflect": jnp.clip(0.2 + 0.75 * jax.random.uniform(streams_of[7], (FACETS, BANDS), jnp.float32) ** level_of(streams_of[7], (FACETS, BANDS), ((0, 512),), -0.2, 0.2), 0.2, 0.95),
    }


def facet_normals(angles):
    azimuth = angles[0]
    elevation = angles[1]
    return jnp.stack([jnp.cos(azimuth) * jnp.cos(elevation), jnp.sin(azimuth) * jnp.cos(elevation), jnp.sin(elevation)])


def view_tile(row_pos, row_nrm, col_pos, col_nrm, col_area, mask):
    along_x = col_pos[0][None, :] - row_pos[0][:, None]
    along_y = col_pos[1][None, :] - row_pos[1][:, None]
    along_z = col_pos[2][None, :] - row_pos[2][:, None]
    cos_row = row_nrm[0][:, None] * along_x + row_nrm[1][:, None] * along_y + row_nrm[2][:, None] * along_z
    cos_col = -(col_nrm[0][None, :] * along_x + col_nrm[1][None, :] * along_y + col_nrm[2][None, :] * along_z)
    dist_sq = along_x * along_x + along_y * along_y + along_z * along_z + col_area[None, :] / math.pi
    return mask * jnp.maximum(cos_row, 0.0) * jnp.maximum(cos_col, 0.0) * col_area[None, :] / (math.pi * dist_sq * dist_sq)


def reference(b_old, positions, angles, areas, visible, assign, emission, reflect):
    normal = facet_normals(angles)
    step_rows = math.gcd(FACETS, 1024)
    count_rows = FACETS // step_rows

    def one_block(index):
        start = (index * step_rows).astype(jnp.int32)
        row_pos = lax.dynamic_slice_in_dim(positions, start, step_rows, 1)
        row_nrm = lax.dynamic_slice_in_dim(normal, start, step_rows, 1)
        row_ids = lax.dynamic_slice_in_dim(assign, start, step_rows, 0)
        mask = visible[row_ids][:, assign].astype(jnp.float32)
        tile = view_tile(row_pos, row_nrm, positions, normal, areas, mask)
        return jnp.dot(tile, b_old, precision=lax.Precision.HIGHEST, preferred_element_type=jnp.float32)

    pieces = lax.map(one_block, jnp.arange(count_rows, dtype=jnp.int32))
    gathered = pieces.reshape(FACETS, BANDS)
    return emission + reflect * gathered
```

```python
import math

import jax
import jax.numpy as jnp
from jax import lax
from jax.experimental import pallas as pl
from jax.experimental.pallas import tpu as pltpu
from jax.sharding import PartitionSpec as P

F32 = jnp.float32
BF16 = jnp.bfloat16
MESH = pl.DeviceIdType.MESH

ROWS = 2048
COLS = 4096
BANDS = 128
PIECE = 256
TILE = 512
STEPS = COLS // TILE
PIECES = ROWS // PIECE
WIDE = 512
CLOSED = 64.0

SIN = (-1 / 6, 1 / 120, -1 / 5040, 1 / 362880, -1 / 39916800, 1 / 6227020800)
COS = (-1 / 2, 1 / 24, -1 / 720, 1 / 40320, -1 / 3628800, 1 / 479001600, -1 / 87178291200)


def sin_cos(angle):
    turns = jnp.floor(angle * (1 / math.pi) + 0.5)
    rest = (angle - turns * 3.140625) - turns * (math.pi - 3.140625)
    sign = 1.0 - 2.0 * (turns * turns)
    square = rest * rest
    odd = jnp.full_like(angle, SIN[-1])
    for factor in SIN[-2::-1]:
        odd = odd * square + factor
    even = jnp.full_like(angle, COS[-1])
    for factor in COS[-2::-1]:
        even = even * square + factor
    return sign * (rest + rest * (square * odd)), sign * (1.0 + square * even)


def rounded(x):
    return x.astype(BF16).astype(F32)


def pieces(x):
    first = rounded(x)
    rest = x - first
    second = rounded(rest)
    return first, second, rounded(rest - second)


def facets(block):
    place = lax.broadcasted_iota(jnp.int32, block.shape, 0)
    pos = jnp.where(place < 3, block, 0.0)
    sine, cosine = sin_cos(block)
    flat = cosine[4:5]
    normal = jnp.where(
        place == 0,
        cosine[3:4] * flat,
        jnp.where(place == 1, sine[3:4] * flat, jnp.where(place == 2, sine[4:5], 0.0)),
    )
    return place, pos, normal


def stacked(place, *lines):
    out = jnp.zeros(place.shape, F32)
    for index, line in enumerate(lines):
        out = jnp.where(place == index, line, out)
    return out


def kernel(
    table,
    b_hbm,
    visible,
    emission,
    reflect,
    out,
    b_full,
    b_two,
    one_of,
    two_of,
    dist_of,
    lhs,
    row_table,
    acc,
    one_a,
    two_a,
    dist_a,
    one_b,
    two_b,
    dist_b,
    sent,
    came,
    first_half,
    second_half,
    core_came,
    z_sent,
    z_came,
    load_sem,
    spread_send,
    spread_recv,
    ring_send,
    ring_recv,
    core_send,
    core_recv,
    z_send,
    z_recv,
):
    row = lax.axis_index("row")
    col = lax.axis_index("col")
    x = col // 4
    z_hi = col // 2 % 2
    core = col % 2
    y = row // 4
    z_lo = row % 4

    load = pltpu.make_async_copy(b_hbm, b_full, load_sem)
    load.start()

    target = (2 * col + z_lo % 2, y // 2 * 4 + z_lo // 2 * 2 + (1 - y % 2))
    source = ((2 * x + (1 - core)) * 4 + z_hi * 2 + row % 2, row // 2)
    right = (row, (x + 1) % 4 * 4 + col % 4)
    left = (row, (x + 3) % 4 * 4 + col % 4)
    sibling = (row, x * 4 + z_hi * 2 + (1 - core))
    across = (row, x * 4 + (1 - z_hi) * 2 + core)

    barrier = pltpu.get_barrier_semaphore()
    for partner in (source, right, left, sibling, across):
        pl.semaphore_signal(barrier, inc=1, device_id=partner, device_id_type=MESH)
    pl.semaphore_wait(barrier, 5)

    half = pl.multiple_of(z_lo % 2 * ROWS, ROWS)
    spread = pltpu.make_async_remote_copy(
        src_ref=table.at[:, pl.ds(half, ROWS)],
        dst_ref=row_table,
        send_sem=spread_send,
        recv_sem=spread_recv,
        device_id=target,
        device_id_type=MESH,
    )
    spread.start()

    shut = ((visible[...].astype(F32) - 1.0) * CLOSED).astype(BF16)

    def column_tables(step, carry):
        lanes = pl.ds(pl.multiple_of(step * WIDE, WIDE), WIDE)
        block = table[:, lanes]
        place, pos, normal = facets(block)
        alpha = block[5:6] * (1 / math.pi)
        weighted = normal * alpha
        offset = -jnp.sum(weighted * pos, axis=0, keepdims=True)
        reach = jnp.sum(pos * pos, axis=0, keepdims=True) + alpha
        p1, p2, p3 = pieces(pos)
        m1, m2, m3 = pieces(weighted)
        t1, t2, t3 = pieces(offset)
        w1, w2, w3 = pieces(reach)
        zero = jnp.zeros_like(block)
        ones = jnp.where(place < 3, 1.0, zero)
        one_of[0:128, lanes] = jnp.concatenate(
            [p1, p2, p3, p1, p2, p1, ones] + [zero] * 9, axis=0
        ).astype(BF16)
        two_of[:, lanes] = jnp.concatenate(
            [zero] * 7 + [m1, m2, m3, m1, m2, m1, stacked(place, t1, t2, t3), zero, zero], axis=0
        ).astype(BF16)
        d1, d2, d3 = -2.0 * p1, -2.0 * p2, -2.0 * p3
        dist_of[:, lanes] = jnp.concatenate(
            [zero] * 7
            + [d1, d2, d3, d1, d2, d1, stacked(place, w1, w2, w3, 1.0, 1.0, 1.0), zero, zero],
            axis=0,
        ).astype(BF16)
        ids = block[6:7].astype(jnp.int32)
        block_ids = lax.broadcasted_iota(jnp.int32, (128, WIDE), 0)
        onehot = jnp.where(block_ids == ids, 1.0, 0.0).astype(BF16)
        one_of[128:256, lanes] = jnp.dot(shut, onehot, preferred_element_type=F32).astype(BF16)
        return carry

    lax.fori_loop(0, COLS // WIDE, column_tables, 0)

    load.wait()

    def split_radiosity(step, carry):
        rows = pl.ds(pl.multiple_of(step * 256, 256), 256)
        value = b_full[rows, :]
        high = value.astype(BF16)
        b_two[rows, 0:128] = high
        b_two[rows, 128:256] = (value - high.astype(F32)).astype(BF16)
        return carry

    lax.fori_loop(0, COLS // 256, split_radiosity, 0)

    spread.wait_recv()

    def row_tables(step, carry):
        lanes = pl.ds(pl.multiple_of(step * 128, 128), 128)
        block = row_table[:, lanes]
        place, pos, normal = facets(block)
        start = -jnp.sum(normal * pos, axis=0, keepdims=True)
        reach = jnp.sum(pos * pos, axis=0, keepdims=True)
        q1, q2, q3 = pieces(pos)
        n1, n2, n3 = pieces(normal)
        s1, s2, s3 = pieces(start)
        r1, r2, r3 = pieces(reach)
        zero = jnp.zeros_like(block)
        groups = [n1, n1, n1, n2, n2, n3, stacked(place, s1, s2, s3)]
        groups += [q1, q1, q1, q2, q2, q3, stacked(place, 1.0, 1.0, 1.0, r1, r2, r3), zero, zero]
        lhs[lanes, 0:128] = jnp.concatenate(groups, axis=0).T.astype(BF16)
        ids = block[6:7].astype(jnp.int32)
        block_ids = lax.broadcasted_iota(jnp.int32, (128, 128), 0)
        lhs[lanes, 128:256] = jnp.where(block_ids == ids, 1.0, 0.0).T.astype(BF16)
        return carry

    lax.fori_loop(0, ROWS // 128, row_tables, 0)

    def half_of(piece):
        return jnp.where(piece < 6, piece % 2, jnp.where(piece == 6, 1 - z_hi, z_hi))

    def first_row(piece):
        side = half_of(piece)
        hop = piece // 2
        owner = jnp.where(side == 0, x + 3 - hop, x + 1 + hop) % 4
        return pl.multiple_of(owner * 512 + side * PIECE, PIECE)

    slots = ((one_a, two_a, dist_a), (one_b, two_b, dist_b))

    def geometry(begin, tile, slot):
        rows = pl.ds(begin, PIECE)
        lanes = pl.ds(pl.multiple_of(tile * TILE, TILE), TILE)
        slot[0][...] = jnp.dot(lhs[rows, :], one_of[:, lanes], preferred_element_type=F32)
        slot[1][...] = jnp.dot(lhs[rows, 0:128], two_of[:, lanes], preferred_element_type=F32)
        slot[2][...] = jnp.dot(lhs[rows, 0:128], dist_of[:, lanes], preferred_element_type=F32)

    def view(slot):
        for lane in range(0, TILE, 128):
            for line in range(0, PIECE, 16):
                part = (slice(line, line + 16), slice(lane, lane + 128))
                dist = slot[2][part]
                both = jnp.maximum(slot[0][part], 0.0) * jnp.maximum(slot[1][part], 0.0)
                slot[2][part] = both * pl.reciprocal(dist * dist, approx=True)

    def gather(tile, slot):
        value = slot[2][...]
        high = value.astype(BF16)
        low = (value - high.astype(F32)).astype(BF16)
        rad = b_two[pl.ds(pl.multiple_of(tile * TILE, TILE), TILE), :]
        total = jnp.dot(high, rad, preferred_element_type=F32)
        total += jnp.dot(low, rad, preferred_element_type=F32)
        acc[...] += total

    def ring(piece):
        return pltpu.make_async_remote_copy(
            src_ref=sent.at[piece],
            dst_ref=came.at[piece],
            send_sem=ring_send.at[piece],
            recv_sem=ring_recv.at[piece],
            device_id=(row, (x + jnp.where(piece % 2 == 0, 1, 3)) % 4 * 4 + col % 4),
            device_id_type=MESH,
        )

    other_rows = pl.ds(pl.multiple_of((1 - core) * 128, 128), 128)
    own_rows = pl.ds(pl.multiple_of(core * 128, 128), 128)

    def core_copy(index, source_ref):
        return pltpu.make_async_remote_copy(
            src_ref=source_ref.at[other_rows],
            dst_ref=core_came.at[index],
            send_sem=core_send.at[index],
            recv_sem=core_recv.at[index],
            device_id=sibling,
            device_id_type=MESH,
        )

    z_copy = pltpu.make_async_remote_copy(
        src_ref=z_sent,
        dst_ref=z_came,
        send_sem=z_send,
        recv_sem=z_recv,
        device_id=across,
        device_id_type=MESH,
    )

    def folded():
        return acc[:, 0:128] + acc[:, 128:256]

    pairs = STEPS // 2
    acc[...] = jnp.zeros_like(acc)
    geometry(first_row(0), 0, slots[0])

    def visit(index, carry):
        piece = index // pairs
        tile = index % pairs * 2
        begin = first_row(piece)
        after = jnp.minimum(index + 1, PIECES * pairs - 1)
        geometry(begin, tile + 1, slots[1])
        view(slots[0])
        gather(tile, slots[0])
        geometry(first_row(after // pairs), after % pairs * 2, slots[0])
        view(slots[1])
        gather(tile + 1, slots[1])

        @pl.when(tile == STEPS - 2)
        def _():
            @pl.when(piece < 2)
            def _():
                sent[piece] = folded()
                ring(piece).start()

            @pl.when((piece >= 2) & (piece < 6))
            def _():
                ring(piece - 2).wait_recv()
                sent[piece] = folded() + came[piece - 2]
                ring(piece).start()

            @pl.when(piece == 6)
            def _():
                ring(5 - z_hi).wait_recv()
                first_half[...] = folded() + came[5 - z_hi]
                core_copy(0, first_half).start()

            @pl.when(piece < 7)
            def _():
                acc[...] = jnp.zeros_like(acc)

        @pl.when((piece == 7) & (tile == 2))
        def _():
            core_copy(0, first_half).wait_recv()
            z_sent[...] = first_half[own_rows, :] + core_came[0]
            z_copy.start()

        return carry

    lax.fori_loop(0, PIECES * pairs, visit, 0)

    ring(4 + z_hi).wait_recv()
    second_half[...] = folded() + came[4 + z_hi]
    core_copy(1, second_half).start()
    z_copy.wait_recv()
    partial = second_half[own_rows, :] + z_came[...]
    core_copy(1, second_half).wait_recv()
    out[...] = emission[...] + reflect[...] * (partial + core_came[1])

    spread.wait_send()
    for piece in range(6):
        ring(piece).wait_send()
    core_copy(0, first_half).wait_send()
    core_copy(1, second_half).wait_send()
    z_copy.wait_send()


def on_device(b_old, positions, angles, areas, visible, assign, emission, reflect):
    table = jnp.concatenate(
        [
            positions,
            angles,
            areas[None, :],
            assign.astype(F32)[None, :],
            jnp.zeros((1, areas.shape[0]), F32),
        ],
        axis=0,
    )
    vmem = pl.BlockSpec(memory_space=pltpu.VMEM)
    return pl.pallas_call(
        kernel,
        out_shape=jax.ShapeDtypeStruct((128, BANDS), F32),
        in_specs=[vmem, pl.BlockSpec(memory_space=pl.ANY), vmem, vmem, vmem],
        out_specs=vmem,
        scratch_shapes=[
            pltpu.VMEM((COLS, BANDS), F32),
            pltpu.VMEM((COLS, 2 * BANDS), BF16),
            pltpu.VMEM((256, COLS), BF16),
            pltpu.VMEM((128, COLS), BF16),
            pltpu.VMEM((128, COLS), BF16),
            pltpu.VMEM((ROWS, 256), BF16),
            pltpu.VMEM((8, ROWS), F32),
            pltpu.VMEM((PIECE, 2 * BANDS), F32),
        ]
        + [pltpu.VMEM((PIECE, TILE), F32)] * 6
        + [
            pltpu.VMEM((6, PIECE, BANDS), F32),
            pltpu.VMEM((6, PIECE, BANDS), F32),
            pltpu.VMEM((PIECE, BANDS), F32),
            pltpu.VMEM((PIECE, BANDS), F32),
            pltpu.VMEM((2, 128, BANDS), F32),
            pltpu.VMEM((128, BANDS), F32),
            pltpu.VMEM((128, BANDS), F32),
            pltpu.SemaphoreType.DMA,
            pltpu.SemaphoreType.DMA,
            pltpu.SemaphoreType.DMA,
            pltpu.SemaphoreType.DMA((6,)),
            pltpu.SemaphoreType.DMA((6,)),
            pltpu.SemaphoreType.DMA((2,)),
            pltpu.SemaphoreType.DMA((2,)),
            pltpu.SemaphoreType.DMA,
            pltpu.SemaphoreType.DMA,
        ],
        compiler_params=pltpu.CompilerParams(
            collective_id=0, has_side_effects=True, vmem_limit_bytes=48 * 2**20
        ),
        name="radiosity",
    )(table, b_old, visible, emission, reflect)


def solution(mesh):
    return jax.shard_map(
        on_device,
        mesh=mesh,
        in_specs=(
            P("col", None),
            P(None, "col"),
            P(None, "col"),
            P("col"),
            P(),
            P("col"),
            P(("row", "col"), None),
            P(("row", "col"), None),
        ),
        out_specs=P(("row", "col"), None),
        check_vma=False,
    )
```

```python
import math

import jax
import jax.numpy as jnp
from jax import lax
from jax.experimental import pallas as pl
from jax.experimental.pallas import tpu as pltpu
from jax.sharding import PartitionSpec as P

F32 = jnp.float32
BF16 = jnp.bfloat16
MESH = pl.DeviceIdType.MESH

ROWS = 2048
COLS = 4096
BANDS = 128
PIECE = 256
TILE = 512
STEPS = COLS // TILE
PIECES = ROWS // PIECE
WIDE = 512
CLOSED = 64.0

SIN = (-1 / 6, 1 / 120, -1 / 5040, 1 / 362880, -1 / 39916800, 1 / 6227020800)
COS = (-1 / 2, 1 / 24, -1 / 720, 1 / 40320, -1 / 3628800, 1 / 479001600, -1 / 87178291200)


def sin_cos(angle):
    turns = jnp.floor(angle * (1 / math.pi) + 0.5)
    rest = (angle - turns * 3.140625) - turns * (math.pi - 3.140625)
    sign = 1.0 - 2.0 * (turns * turns)
    square = rest * rest
    odd = jnp.full_like(angle, SIN[-1])
    for factor in SIN[-2::-1]:
        odd = odd * square + factor
    even = jnp.full_like(angle, COS[-1])
    for factor in COS[-2::-1]:
        even = even * square + factor
    return sign * (rest + rest * (square * odd)), sign * (1.0 + square * even)


def rounded(x):
    return x.astype(BF16).astype(F32)


def pieces(x):
    first = rounded(x)
    rest = x - first
    second = rounded(rest)
    return first, second, rounded(rest - second)


def facets(block):
    place = lax.broadcasted_iota(jnp.int32, block.shape, 0)
    pos = jnp.where(place < 3, block, 0.0)
    sine, cosine = sin_cos(block)
    flat = cosine[4:5]
    normal = jnp.where(
        place == 0,
        cosine[3:4] * flat,
        jnp.where(place == 1, sine[3:4] * flat, jnp.where(place == 2, sine[4:5], 0.0)),
    )
    return place, pos, normal


def stacked(place, *lines):
    out = jnp.zeros(place.shape, F32)
    for index, line in enumerate(lines):
        out = jnp.where(place == index, line, out)
    return out


def kernel(
    positions_hbm,
    angles_hbm,
    areas_hbm,
    assign_hbm,
    b_hbm,
    visible_hbm,
    emission_hbm,
    reflect_hbm,
    out,
    positions,
    angles,
    areas,
    assign,
    table,
    b_full,
    visible,
    emission,
    reflect,
    b_two,
    one_of,
    two_of,
    dist_of,
    lhs,
    row_table,
    acc,
    one_a,
    two_a,
    dist_a,
    one_b,
    two_b,
    dist_b,
    view_a,
    view_b,
    sent,
    came,
    first_half,
    second_half,
    core_came,
    z_sent,
    z_came,
    load_sem,
    spread_send,
    spread_recv,
    ring_send,
    ring_recv,
    core_send,
    core_recv,
    z_send,
    z_recv,
):
    row = lax.axis_index("row")
    col = lax.axis_index("col")
    x = col // 4
    z_hi = col // 2 % 2
    core = col % 2
    y = row // 4
    z_lo = row % 4

    loads = [
        pltpu.make_async_copy(source, target, load_sem.at[index])
        for index, (source, target) in enumerate(
            (
                (positions_hbm, positions),
                (angles_hbm, angles),
                (areas_hbm, areas),
                (assign_hbm, assign),
                (visible_hbm, visible),
                (b_hbm, b_full),
                (emission_hbm, emission),
                (reflect_hbm, reflect),
            )
        )
    ]
    for load in loads:
        load.start()

    target = (2 * col + z_lo % 2, y // 2 * 4 + z_lo // 2 * 2 + (1 - y % 2))
    source = ((2 * x + (1 - core)) * 4 + z_hi * 2 + row % 2, row // 2)
    right = (row, (x + 1) % 4 * 4 + col % 4)
    left = (row, (x + 3) % 4 * 4 + col % 4)
    sibling = (row, x * 4 + z_hi * 2 + (1 - core))
    across = (row, x * 4 + (1 - z_hi) * 2 + core)

    barrier = pltpu.get_barrier_semaphore()
    for partner in (source, right, left, sibling, across):
        pl.semaphore_signal(barrier, inc=1, device_id=partner, device_id_type=MESH)
    for load in loads[0:4]:
        load.wait()
    table[0:3, :] = positions[...]
    table[3:5, :] = angles[...]
    table[5:6, :] = areas[...]
    table[6:7, :] = assign[...].astype(F32)
    table[7:8, :] = jnp.zeros((1, COLS), F32)
    pl.semaphore_wait(barrier, 5)

    half = pl.multiple_of(z_lo % 2 * ROWS, ROWS)
    spread = pltpu.make_async_remote_copy(
        src_ref=table.at[:, pl.ds(half, ROWS)],
        dst_ref=row_table,
        send_sem=spread_send,
        recv_sem=spread_recv,
        device_id=target,
        device_id_type=MESH,
    )
    spread.start()

    loads[4].wait()
    shut = ((visible[...].astype(F32) - 1.0) * CLOSED).astype(BF16)

    def column_tables(step, carry):
        lanes = pl.ds(pl.multiple_of(step * WIDE, WIDE), WIDE)
        block = table[:, lanes]
        place, pos, normal = facets(block)
        alpha = block[5:6] * (1 / math.pi)
        weighted = normal * alpha
        offset = -jnp.sum(weighted * pos, axis=0, keepdims=True)
        reach = jnp.sum(pos * pos, axis=0, keepdims=True) + alpha
        p1, p2, p3 = pieces(pos)
        m1, m2, m3 = pieces(weighted)
        t1, t2, t3 = pieces(offset)
        w1, w2, w3 = pieces(reach)
        zero = jnp.zeros_like(block)
        ones = jnp.where(place < 3, 1.0, zero)
        one_of[0:128, lanes] = jnp.concatenate(
            [zero] * 8 + [p1, p2, p3, p1, p2, p1, ones, zero], axis=0
        ).astype(BF16)
        two_of[:, lanes] = jnp.concatenate(
            [m1, m2, m3, m1, m2, m1, stacked(place, t1, t2, t3), zero], axis=0
        ).astype(BF16)
        d1, d2, d3 = -2.0 * p1, -2.0 * p2, -2.0 * p3
        dist_of[:, lanes] = jnp.concatenate(
            [d1, d2, d3, d1, d2, d1, stacked(place, w1, w2, w3, 1.0, 1.0, 1.0), zero],
            axis=0,
        ).astype(BF16)
        ids = block[6:7].astype(jnp.int32)
        block_ids = lax.broadcasted_iota(jnp.int32, (128, WIDE), 0)
        onehot = jnp.where(block_ids == ids, 1.0, 0.0).astype(BF16)
        one_of[128:256, lanes] = jnp.dot(shut, onehot, preferred_element_type=F32).astype(BF16)
        return carry

    lax.fori_loop(0, COLS // WIDE, column_tables, 0)

    loads[5].wait()

    def split_radiosity(step, carry):
        rows = pl.ds(pl.multiple_of(step * 256, 256), 256)
        value = b_full[rows, :]
        high = value.astype(BF16)
        b_two[rows, 0:128] = high
        b_two[rows, 128:256] = (value - high.astype(F32)).astype(BF16)
        return carry

    lax.fori_loop(0, COLS // 256, split_radiosity, 0)

    spread.wait_recv()

    def row_tables(step, carry):
        lanes = pl.ds(pl.multiple_of(step * 128, 128), 128)
        block = row_table[:, lanes]
        place, pos, normal = facets(block)
        start = -jnp.sum(normal * pos, axis=0, keepdims=True)
        reach = jnp.sum(pos * pos, axis=0, keepdims=True)
        q1, q2, q3 = pieces(pos)
        n1, n2, n3 = pieces(normal)
        s1, s2, s3 = pieces(start)
        r1, r2, r3 = pieces(reach)
        zero = jnp.zeros_like(block)
        groups = [q1, q1, q1, q2, q2, q3, stacked(place, 1.0, 1.0, 1.0, r1, r2, r3), zero]
        groups += [n1, n1, n1, n2, n2, n3, stacked(place, s1, s2, s3), zero]
        lhs[lanes, 0:128] = jnp.concatenate(groups, axis=0).T.astype(BF16)
        ids = block[6:7].astype(jnp.int32)
        block_ids = lax.broadcasted_iota(jnp.int32, (128, 128), 0)
        lhs[lanes, 128:256] = jnp.where(block_ids == ids, 1.0, 0.0).T.astype(BF16)
        return carry

    lax.fori_loop(0, ROWS // 128, row_tables, 0)

    def half_of(piece):
        return jnp.where(piece < 6, piece % 2, jnp.where(piece == 6, 1 - z_hi, z_hi))

    def first_row(piece):
        side = half_of(piece)
        hop = piece // 2
        owner = jnp.where(side == 0, x + 3 - hop, x + 1 + hop) % 4
        return pl.multiple_of(owner * 512 + side * PIECE, PIECE)

    slots = ((one_a, two_a, dist_a), (one_b, two_b, dist_b))

    def geometry(begin, tile, slot):
        rows = pl.ds(begin, PIECE)
        lanes = pl.ds(pl.multiple_of(tile * TILE, TILE), TILE)
        slot[0][...] = jnp.dot(lhs[rows, :], one_of[:, lanes], preferred_element_type=F32)
        slot[1][...] = jnp.dot(lhs[rows, 0:64], two_of[:, lanes], preferred_element_type=F32)
        slot[2][...] = jnp.dot(lhs[rows, 0:64], dist_of[:, lanes], preferred_element_type=F32)

    def view(slot, views):
        for lane in range(0, TILE, 128):
            for line in range(0, PIECE, 16):
                part = (slice(line, line + 16), slice(lane, lane + 128))
                dist = slot[2][part]
                both = jnp.maximum(slot[0][part], 0.0) * jnp.maximum(slot[1][part], 0.0)
                views[part] = both * pl.reciprocal(dist * dist, approx=True)

    def gather(tile, views):
        value = views[...]
        high = value.astype(BF16)
        low = (value - high.astype(F32)).astype(BF16)
        rad = b_two[pl.ds(pl.multiple_of(tile * TILE, TILE), TILE), :]
        total = jnp.dot(high, rad, preferred_element_type=F32)
        total += jnp.dot(low, rad, preferred_element_type=F32)
        acc[...] += total

    def ring(piece):
        return pltpu.make_async_remote_copy(
            src_ref=sent.at[piece],
            dst_ref=came.at[piece],
            send_sem=ring_send.at[piece],
            recv_sem=ring_recv.at[piece],
            device_id=(row, (x + jnp.where(piece % 2 == 0, 1, 3)) % 4 * 4 + col % 4),
            device_id_type=MESH,
        )

    other_rows = pl.ds(pl.multiple_of((1 - core) * 128, 128), 128)
    own_rows = pl.ds(pl.multiple_of(core * 128, 128), 128)

    def core_copy(index, source_ref):
        return pltpu.make_async_remote_copy(
            src_ref=source_ref.at[other_rows],
            dst_ref=core_came.at[index],
            send_sem=core_send.at[index],
            recv_sem=core_recv.at[index],
            device_id=sibling,
            device_id_type=MESH,
        )

    z_copy = pltpu.make_async_remote_copy(
        src_ref=z_sent,
        dst_ref=z_came,
        send_sem=z_send,
        recv_sem=z_recv,
        device_id=across,
        device_id_type=MESH,
    )

    def folded():
        return acc[:, 0:128] + acc[:, 128:256]

    pairs = STEPS // 2
    tiles = PIECES * STEPS
    acc[...] = jnp.zeros_like(acc)

    def geometry_of(index, slot):
        geometry(first_row(index // STEPS), index % STEPS, slot)

    geometry_of(0, slots[0])
    view(slots[0], view_a)
    geometry_of(1, slots[1])

    def visit(index, carry):
        piece = index // pairs
        tile = index % pairs * 2
        after = jnp.minimum(index * 2 + 2, tiles - 2)
        geometry_of(after, slots[0])
        view(slots[1], view_b)
        gather(tile, view_a)
        geometry_of(after + 1, slots[1])
        view(slots[0], view_a)
        gather(tile + 1, view_b)

        @pl.when(tile == STEPS - 2)
        def _():
            @pl.when(piece < 2)
            def _():
                sent[piece] = folded()
                ring(piece).start()

            @pl.when((piece >= 2) & (piece < 6))
            def _():
                ring(piece - 2).wait_recv()
                sent[piece] = folded() + came[piece - 2]
                ring(piece).start()

            @pl.when(piece == 6)
            def _():
                ring(5 - z_hi).wait_recv()
                first_half[...] = folded() + came[5 - z_hi]
                core_copy(0, first_half).start()

            @pl.when(piece < 7)
            def _():
                acc[...] = jnp.zeros_like(acc)

        @pl.when((piece == 7) & (tile == 2))
        def _():
            core_copy(0, first_half).wait_recv()
            z_sent[...] = first_half[own_rows, :] + core_came[0]
            z_copy.start()

        return carry

    lax.fori_loop(0, PIECES * pairs, visit, 0)

    ring(4 + z_hi).wait_recv()
    second_half[...] = folded() + came[4 + z_hi]
    core_copy(1, second_half).start()
    z_copy.wait_recv()
    partial = second_half[own_rows, :] + z_came[...]
    core_copy(1, second_half).wait_recv()
    loads[6].wait()
    loads[7].wait()
    out[...] = emission[...] + reflect[...] * (partial + core_came[1])

    spread.wait_send()
    for piece in range(6):
        ring(piece).wait_send()
    core_copy(0, first_half).wait_send()
    core_copy(1, second_half).wait_send()
    z_copy.wait_send()


def on_device(b_old, positions, angles, areas, visible, assign, emission, reflect):
    vmem = pl.BlockSpec(memory_space=pltpu.VMEM)
    return pl.pallas_call(
        kernel,
        out_shape=jax.ShapeDtypeStruct((128, BANDS), F32),
        in_specs=[pl.BlockSpec(memory_space=pl.ANY)] * 8,
        out_specs=vmem,
        scratch_shapes=[
            pltpu.VMEM((3, COLS), F32),
            pltpu.VMEM((2, COLS), F32),
            pltpu.VMEM((1, COLS), F32),
            pltpu.VMEM((1, COLS), jnp.int32),
            pltpu.VMEM((8, COLS), F32),
            pltpu.VMEM((COLS, BANDS), F32),
            pltpu.VMEM((128, 128), jnp.int32),
            pltpu.VMEM((128, BANDS), F32),
            pltpu.VMEM((128, BANDS), F32),
            pltpu.VMEM((COLS, 2 * BANDS), BF16),
            pltpu.VMEM((256, COLS), BF16),
            pltpu.VMEM((64, COLS), BF16),
            pltpu.VMEM((64, COLS), BF16),
            pltpu.VMEM((ROWS, 256), BF16),
            pltpu.VMEM((8, ROWS), F32),
            pltpu.VMEM((PIECE, 2 * BANDS), F32),
        ]
        + [pltpu.VMEM((PIECE, TILE), F32)] * 8
        + [
            pltpu.VMEM((6, PIECE, BANDS), F32),
            pltpu.VMEM((6, PIECE, BANDS), F32),
            pltpu.VMEM((PIECE, BANDS), F32),
            pltpu.VMEM((PIECE, BANDS), F32),
            pltpu.VMEM((2, 128, BANDS), F32),
            pltpu.VMEM((128, BANDS), F32),
            pltpu.VMEM((128, BANDS), F32),
            pltpu.SemaphoreType.DMA((8,)),
            pltpu.SemaphoreType.DMA,
            pltpu.SemaphoreType.DMA,
            pltpu.SemaphoreType.DMA((6,)),
            pltpu.SemaphoreType.DMA((6,)),
            pltpu.SemaphoreType.DMA((2,)),
            pltpu.SemaphoreType.DMA((2,)),
            pltpu.SemaphoreType.DMA,
            pltpu.SemaphoreType.DMA,
        ],
        compiler_params=pltpu.CompilerParams(
            collective_id=0, has_side_effects=True, vmem_limit_bytes=60 * 2**20
        ),
        name="radiosity",
    )(
        positions,
        angles,
        areas[None, :],
        assign[None, :],
        b_old,
        visible,
        emission,
        reflect,
    )


def solution(mesh):
    return jax.shard_map(
        on_device,
        mesh=mesh,
        in_specs=(
            P("col", None),
            P(None, "col"),
            P(None, "col"),
            P("col"),
            P(),
            P("col"),
            P(("row", "col"), None),
            P(("row", "col"), None),
        ),
        out_specs=P(("row", "col"), None),
        check_vma=False,
    )
```

```python
import math

import jax
import jax.numpy as jnp
from jax import lax
from jax.experimental import pallas as pl
from jax.experimental.pallas import tpu as pltpu
from jax.sharding import PartitionSpec as P

F32 = jnp.float32
BF16 = jnp.bfloat16
MESH = pl.DeviceIdType.MESH

ROWS = 2048
COLS = 4096
BANDS = 128
PIECE = 256
TILE = 512
STEPS = COLS // TILE
PIECES = ROWS // PIECE
WIDE = 512
CLOSED = 64.0

SIN = (-1 / 6, 1 / 120, -1 / 5040, 1 / 362880, -1 / 39916800, 1 / 6227020800)
COS = (-1 / 2, 1 / 24, -1 / 720, 1 / 40320, -1 / 3628800, 1 / 479001600, -1 / 87178291200)


def sin_cos(angle):
    turns = jnp.floor(angle * (1 / math.pi) + 0.5)
    rest = (angle - turns * 3.140625) - turns * (math.pi - 3.140625)
    sign = 1.0 - 2.0 * (turns * turns)
    square = rest * rest
    odd = jnp.full_like(angle, SIN[-1])
    for factor in SIN[-2::-1]:
        odd = odd * square + factor
    even = jnp.full_like(angle, COS[-1])
    for factor in COS[-2::-1]:
        even = even * square + factor
    return sign * (rest + rest * (square * odd)), sign * (1.0 + square * even)


def rounded(x):
    return x.astype(BF16).astype(F32)


def pieces(x):
    first = rounded(x)
    rest = x - first
    second = rounded(rest)
    return first, second, rounded(rest - second)


def facets(block):
    place = lax.broadcasted_iota(jnp.int32, block.shape, 0)
    pos = jnp.where(place < 3, block, 0.0)
    sine, cosine = sin_cos(block)
    flat = cosine[4:5]
    normal = jnp.where(
        place == 0,
        cosine[3:4] * flat,
        jnp.where(place == 1, sine[3:4] * flat, jnp.where(place == 2, sine[4:5], 0.0)),
    )
    return place, pos, normal


def stacked(place, *lines):
    out = jnp.zeros(place.shape, F32)
    for index, line in enumerate(lines):
        out = jnp.where(place == index, line, out)
    return out


def kernel(
    positions_hbm,
    angles_hbm,
    areas_hbm,
    assign_hbm,
    b_hbm,
    visible_hbm,
    emission_hbm,
    reflect_hbm,
    out,
    positions,
    angles,
    areas,
    assign,
    table,
    b_full,
    visible,
    emission,
    reflect,
    b_two,
    one_of,
    two_of,
    dist_of,
    lhs,
    row_table,
    acc,
    one_a,
    two_a,
    dist_a,
    one_b,
    two_b,
    dist_b,
    view_a,
    view_b,
    sent,
    came,
    first_half,
    second_half,
    core_came,
    z_sent,
    z_came,
    load_sem,
    spread_send,
    forward_send,
    spread_recv,
    ring_send,
    ring_recv,
    core_send,
    core_recv,
    z_send,
    z_recv,
):
    row = lax.axis_index("row")
    col = lax.axis_index("col")
    x = col // 4
    z_hi = col // 2 % 2
    core = col % 2
    is_source = col == row // 2
    serves = core == row // 2 % 2
    is_leader = serves & jnp.logical_not(is_source)

    loads = [
        pltpu.make_async_copy(source, target, load_sem.at[index])
        for index, (source, target) in enumerate(
            (
                (positions_hbm, positions),
                (angles_hbm, angles),
                (areas_hbm, areas),
                (assign_hbm, assign),
                (visible_hbm, visible),
                (b_hbm, b_full),
                (emission_hbm, emission),
                (reflect_hbm, reflect),
            )
        )
    ]
    for load in loads:
        load.start()

    right = (row, (x + 1) % 4 * 4 + col % 4)
    left = (row, (x + 3) % 4 * 4 + col % 4)
    sibling = (row, x * 4 + z_hi * 2 + (1 - core))
    across = (row, x * 4 + (1 - z_hi) * 2 + core)

    barrier = pltpu.get_barrier_semaphore()
    for partner in (right, left, sibling, across):
        pl.semaphore_signal(barrier, inc=1, device_id=partner, device_id_type=MESH)

    @pl.when(is_leader)
    def _():
        pl.semaphore_signal(barrier, inc=1, device_id=(row, row // 2), device_id_type=MESH)

    for load in loads[0:4]:
        load.wait()
    table[0:3, :] = positions[...]
    table[3:5, :] = angles[...]
    table[5:6, :] = areas[...]
    table[6:7, :] = assign[...].astype(F32)
    table[7:8, :] = jnp.zeros((1, COLS), F32)
    pl.semaphore_wait(barrier, jnp.where(is_source, 11, 4))

    def spread(hop):
        return pltpu.make_async_remote_copy(
            src_ref=table.at[:, pl.ds(pl.multiple_of(row % 2 * ROWS, ROWS), ROWS)],
            dst_ref=row_table,
            send_sem=spread_send.at[hop - 1],
            recv_sem=spread_recv,
            device_id=(row, (row // 4 + hop) % 8 * 2 + core),
            device_id_type=MESH,
        )

    forward = pltpu.make_async_remote_copy(
        src_ref=row_table,
        dst_ref=row_table,
        send_sem=forward_send,
        recv_sem=spread_recv,
        device_id=sibling,
        device_id_type=MESH,
    )

    @pl.when(is_source)
    def _():
        for hop in (4, 3, 5, 2, 6, 1, 7):
            spread(hop).start()
        row_table[...] = table[:, pl.ds(pl.multiple_of(row % 2 * ROWS, ROWS), ROWS)]
        forward.start()

    loads[4].wait()
    shut = ((visible[...].astype(F32) - 1.0) * CLOSED).astype(BF16)

    def column_tables(step, carry):
        lanes = pl.ds(pl.multiple_of(step * WIDE, WIDE), WIDE)
        block = table[:, lanes]
        place, pos, normal = facets(block)
        alpha = block[5:6] * (1 / math.pi)
        weighted = normal * alpha
        offset = -jnp.sum(weighted * pos, axis=0, keepdims=True)
        reach = jnp.sum(pos * pos, axis=0, keepdims=True) + alpha
        p1, p2, p3 = pieces(pos)
        m1, m2, m3 = pieces(weighted)
        t1, t2, t3 = pieces(offset)
        w1, w2, w3 = pieces(reach)
        zero = jnp.zeros_like(block)
        ones = jnp.where(place < 3, 1.0, zero)
        one_of[0:128, lanes] = jnp.concatenate(
            [zero] * 8 + [p1, p2, p3, p1, p2, p1, ones, zero], axis=0
        ).astype(BF16)
        two_of[:, lanes] = jnp.concatenate(
            [m1, m2, m3, m1, m2, m1, stacked(place, t1, t2, t3), zero], axis=0
        ).astype(BF16)
        d1, d2, d3 = -2.0 * p1, -2.0 * p2, -2.0 * p3
        dist_of[:, lanes] = jnp.concatenate(
            [d1, d2, d3, d1, d2, d1, stacked(place, w1, w2, w3, 1.0, 1.0, 1.0), zero],
            axis=0,
        ).astype(BF16)
        ids = block[6:7].astype(jnp.int32)
        block_ids = lax.broadcasted_iota(jnp.int32, (128, WIDE), 0)
        onehot = jnp.where(block_ids == ids, 1.0, 0.0).astype(BF16)
        one_of[128:256, lanes] = jnp.dot(shut, onehot, preferred_element_type=F32).astype(BF16)
        return carry

    lax.fori_loop(0, COLS // WIDE, column_tables, 0)

    @pl.when(is_leader)
    def _():
        spread(1).wait_recv()
        forward.start()

    loads[5].wait()

    def split_radiosity(step, carry):
        rows = pl.ds(pl.multiple_of(step * 256, 256), 256)
        value = b_full[rows, :]
        high = value.astype(BF16)
        b_two[rows, 0:128] = high
        b_two[rows, 128:256] = (value - high.astype(F32)).astype(BF16)
        return carry

    lax.fori_loop(0, COLS // 256, split_radiosity, 0)

    @pl.when(jnp.logical_not(serves))
    def _():
        forward.wait_recv()


    def row_tables(step, carry):
        lanes = pl.ds(pl.multiple_of(step * 128, 128), 128)
        block = row_table[:, lanes]
        place, pos, normal = facets(block)
        start = -jnp.sum(normal * pos, axis=0, keepdims=True)
        reach = jnp.sum(pos * pos, axis=0, keepdims=True)
        q1, q2, q3 = pieces(pos)
        n1, n2, n3 = pieces(normal)
        s1, s2, s3 = pieces(start)
        r1, r2, r3 = pieces(reach)
        zero = jnp.zeros_like(block)
        groups = [q1, q1, q1, q2, q2, q3, stacked(place, 1.0, 1.0, 1.0, r1, r2, r3), zero]
        groups += [n1, n1, n1, n2, n2, n3, stacked(place, s1, s2, s3), zero]
        lhs[lanes, 0:128] = jnp.concatenate(groups, axis=0).T.astype(BF16)
        ids = block[6:7].astype(jnp.int32)
        block_ids = lax.broadcasted_iota(jnp.int32, (128, 128), 0)
        lhs[lanes, 128:256] = jnp.where(block_ids == ids, 1.0, 0.0).T.astype(BF16)
        return carry

    lax.fori_loop(0, ROWS // 128, row_tables, 0)

    def half_of(piece):
        return jnp.where(piece < 6, piece % 2, jnp.where(piece == 6, 1 - z_hi, z_hi))

    def first_row(piece):
        side = half_of(piece)
        hop = piece // 2
        owner = jnp.where(side == 0, x + 3 - hop, x + 1 + hop) % 4
        return pl.multiple_of(owner * 512 + side * PIECE, PIECE)

    slots = ((one_a, two_a, dist_a), (one_b, two_b, dist_b))

    def geometry(begin, tile, slot):
        rows = pl.ds(begin, PIECE)
        lanes = pl.ds(pl.multiple_of(tile * TILE, TILE), TILE)
        slot[0][...] = jnp.dot(lhs[rows, :], one_of[:, lanes], preferred_element_type=F32)
        slot[1][...] = jnp.dot(lhs[rows, 0:64], two_of[:, lanes], preferred_element_type=F32)
        slot[2][...] = jnp.dot(lhs[rows, 0:64], dist_of[:, lanes], preferred_element_type=F32)

    def view(slot, views):
        for lane in range(0, TILE, 128):
            for line in range(0, PIECE, 16):
                part = (slice(line, line + 16), slice(lane, lane + 128))
                dist = slot[2][part]
                both = jnp.maximum(slot[0][part], 0.0) * jnp.maximum(slot[1][part], 0.0)
                views[part] = both * pl.reciprocal(dist * dist, approx=True)

    def gather(tile, views):
        value = views[...]
        high = value.astype(BF16)
        low = (value - high.astype(F32)).astype(BF16)
        rad = b_two[pl.ds(pl.multiple_of(tile * TILE, TILE), TILE), :]
        total = jnp.dot(high, rad, preferred_element_type=F32)
        total += jnp.dot(low, rad, preferred_element_type=F32)
        acc[...] += total

    def ring(piece):
        return pltpu.make_async_remote_copy(
            src_ref=sent.at[piece],
            dst_ref=came.at[piece],
            send_sem=ring_send.at[piece],
            recv_sem=ring_recv.at[piece],
            device_id=(row, (x + jnp.where(piece % 2 == 0, 1, 3)) % 4 * 4 + col % 4),
            device_id_type=MESH,
        )

    other_rows = pl.ds(pl.multiple_of((1 - core) * 128, 128), 128)
    own_rows = pl.ds(pl.multiple_of(core * 128, 128), 128)

    def core_copy(index, source_ref):
        return pltpu.make_async_remote_copy(
            src_ref=source_ref.at[other_rows],
            dst_ref=core_came.at[index],
            send_sem=core_send.at[index],
            recv_sem=core_recv.at[index],
            device_id=sibling,
            device_id_type=MESH,
        )

    z_copy = pltpu.make_async_remote_copy(
        src_ref=z_sent,
        dst_ref=z_came,
        send_sem=z_send,
        recv_sem=z_recv,
        device_id=across,
        device_id_type=MESH,
    )

    def folded():
        return acc[:, 0:128] + acc[:, 128:256]

    pairs = STEPS // 2
    tiles = PIECES * STEPS
    acc[...] = jnp.zeros_like(acc)

    def geometry_of(index, slot):
        geometry(first_row(index // STEPS), index % STEPS, slot)

    geometry_of(0, slots[0])
    view(slots[0], view_a)
    geometry_of(1, slots[1])

    def visit(index, carry):
        piece = index // pairs
        tile = index % pairs * 2
        after = jnp.minimum(index * 2 + 2, tiles - 2)
        geometry_of(after, slots[0])
        view(slots[1], view_b)
        gather(tile, view_a)
        geometry_of(after + 1, slots[1])
        view(slots[0], view_a)
        gather(tile + 1, view_b)

        @pl.when(tile == STEPS - 2)
        def _():
            @pl.when(piece < 2)
            def _():
                sent[piece] = folded()
                ring(piece).start()

            @pl.when((piece >= 2) & (piece < 6))
            def _():
                ring(piece - 2).wait_recv()
                sent[piece] = folded() + came[piece - 2]
                ring(piece).start()

            @pl.when(piece == 6)
            def _():
                ring(5 - z_hi).wait_recv()
                first_half[...] = folded() + came[5 - z_hi]
                core_copy(0, first_half).start()

            @pl.when(piece < 7)
            def _():
                acc[...] = jnp.zeros_like(acc)

        @pl.when((piece == 7) & (tile == 2))
        def _():
            core_copy(0, first_half).wait_recv()
            z_sent[...] = first_half[own_rows, :] + core_came[0]
            z_copy.start()

        return carry

    lax.fori_loop(0, PIECES * pairs, visit, 0)

    ring(4 + z_hi).wait_recv()
    second_half[...] = folded() + came[4 + z_hi]
    core_copy(1, second_half).start()
    z_copy.wait_recv()
    partial = second_half[own_rows, :] + z_came[...]
    core_copy(1, second_half).wait_recv()
    loads[6].wait()
    loads[7].wait()
    out[...] = emission[...] + reflect[...] * (partial + core_came[1])

    @pl.when(is_source)
    def _():
        for hop in range(1, 8):
            spread(hop).wait_send()

    @pl.when(serves)
    def _():
        forward.wait_send()

    for piece in range(6):
        ring(piece).wait_send()
    core_copy(0, first_half).wait_send()
    core_copy(1, second_half).wait_send()
    z_copy.wait_send()


def on_device(b_old, positions, angles, areas, visible, assign, emission, reflect):
    vmem = pl.BlockSpec(memory_space=pltpu.VMEM)
    return pl.pallas_call(
        kernel,
        out_shape=jax.ShapeDtypeStruct((128, BANDS), F32),
        in_specs=[pl.BlockSpec(memory_space=pl.ANY)] * 8,
        out_specs=vmem,
        scratch_shapes=[
            pltpu.VMEM((3, COLS), F32),
            pltpu.VMEM((2, COLS), F32),
            pltpu.VMEM((1, COLS), F32),
            pltpu.VMEM((1, COLS), jnp.int32),
            pltpu.VMEM((8, COLS), F32),
            pltpu.VMEM((COLS, BANDS), F32),
            pltpu.VMEM((128, 128), jnp.int32),
            pltpu.VMEM((128, BANDS), F32),
            pltpu.VMEM((128, BANDS), F32),
            pltpu.VMEM((COLS, 2 * BANDS), BF16),
            pltpu.VMEM((256, COLS), BF16),
            pltpu.VMEM((64, COLS), BF16),
            pltpu.VMEM((64, COLS), BF16),
            pltpu.VMEM((ROWS, 256), BF16),
            pltpu.VMEM((8, ROWS), F32),
            pltpu.VMEM((PIECE, 2 * BANDS), F32),
        ]
        + [pltpu.VMEM((PIECE, TILE), F32)] * 8
        + [
            pltpu.VMEM((6, PIECE, BANDS), F32),
            pltpu.VMEM((6, PIECE, BANDS), F32),
            pltpu.VMEM((PIECE, BANDS), F32),
            pltpu.VMEM((PIECE, BANDS), F32),
            pltpu.VMEM((2, 128, BANDS), F32),
            pltpu.VMEM((128, BANDS), F32),
            pltpu.VMEM((128, BANDS), F32),
            pltpu.SemaphoreType.DMA((8,)),
            pltpu.SemaphoreType.DMA((7,)),
            pltpu.SemaphoreType.DMA,
            pltpu.SemaphoreType.DMA,
            pltpu.SemaphoreType.DMA((6,)),
            pltpu.SemaphoreType.DMA((6,)),
            pltpu.SemaphoreType.DMA((2,)),
            pltpu.SemaphoreType.DMA((2,)),
            pltpu.SemaphoreType.DMA,
            pltpu.SemaphoreType.DMA,
        ],
        compiler_params=pltpu.CompilerParams(
            collective_id=0, has_side_effects=True, vmem_limit_bytes=60 * 2**20
        ),
        name="radiosity",
    )(
        positions,
        angles,
        areas[None, :],
        assign[None, :],
        b_old,
        visible,
        emission,
        reflect,
    )


def solution(mesh):
    return jax.shard_map(
        on_device,
        mesh=mesh,
        in_specs=(
            P("col", None),
            P(None, "col"),
            P(None, "col"),
            P("col"),
            P(),
            P("col"),
            P(("row", "col"), None),
            P(("row", "col"), None),
        ),
        out_specs=P(("row", "col"), None),
        check_vma=False,
    )
```

```python
import math

import jax
import jax.numpy as jnp
from jax import lax
from jax.experimental import pallas as pl
from jax.experimental.pallas import tpu as pltpu
from jax.sharding import PartitionSpec as P

F32 = jnp.float32
BF16 = jnp.bfloat16
MESH = pl.DeviceIdType.MESH

ROWS = 2048
COLS = 4096
BANDS = 128
PIECE = 256
TILE = 512
STEPS = COLS // TILE
PIECES = ROWS // PIECE
WIDE = 512
CLOSED = 64.0

SIN = (-1 / 6, 1 / 120, -1 / 5040, 1 / 362880, -1 / 39916800, 1 / 6227020800)
COS = (-1 / 2, 1 / 24, -1 / 720, 1 / 40320, -1 / 3628800, 1 / 479001600, -1 / 87178291200)


def sin_cos(angle):
    turns = jnp.floor(angle * (1 / math.pi) + 0.5)
    rest = (angle - turns * 3.140625) - turns * (math.pi - 3.140625)
    sign = 1.0 - 2.0 * (turns * turns)
    square = rest * rest
    odd = jnp.full_like(angle, SIN[-1])
    for factor in SIN[-2::-1]:
        odd = odd * square + factor
    even = jnp.full_like(angle, COS[-1])
    for factor in COS[-2::-1]:
        even = even * square + factor
    return sign * (rest + rest * (square * odd)), sign * (1.0 + square * even)


def rounded(x):
    return x.astype(BF16).astype(F32)


def pieces(x):
    first = rounded(x)
    rest = x - first
    second = rounded(rest)
    return first, second, rounded(rest - second)


def facets(block):
    place = lax.broadcasted_iota(jnp.int32, block.shape, 0)
    pos = jnp.where(place < 3, block, 0.0)
    sine, cosine = sin_cos(block)
    flat = cosine[4:5]
    normal = jnp.where(
        place == 0,
        cosine[3:4] * flat,
        jnp.where(place == 1, sine[3:4] * flat, jnp.where(place == 2, sine[4:5], 0.0)),
    )
    return place, pos, normal


def stacked(place, *lines):
    out = jnp.zeros(place.shape, F32)
    for index, line in enumerate(lines):
        out = jnp.where(place == index, line, out)
    return out


def kernel(
    positions_hbm,
    angles_hbm,
    areas_hbm,
    assign_hbm,
    b_hbm,
    visible_hbm,
    emission_hbm,
    reflect_hbm,
    out,
    positions,
    angles,
    areas,
    assign,
    table,
    b_full,
    visible,
    emission,
    reflect,
    b_two,
    one_of,
    two_of,
    dist_of,
    lhs,
    row_table,
    acc,
    one_a,
    two_a,
    dist_a,
    one_b,
    two_b,
    dist_b,
    view_a,
    view_b,
    sent,
    came,
    first_half,
    second_half,
    core_came,
    z_sent,
    z_came,
    load_sem,
    spread_send,
    over_send,
    forward_send,
    spread_recv,
    ring_send,
    ring_recv,
    core_send,
    core_recv,
    z_send,
    z_recv,
):
    row = lax.axis_index("row")
    col = lax.axis_index("col")
    x = col // 4
    z_hi = col // 2 % 2
    core = col % 2
    home = row // 2
    serves = core == home % 2
    near = serves & (z_hi == home // 2 % 2)
    is_source = col == home
    is_relay = near & jnp.logical_not(is_source)
    is_far = serves & jnp.logical_not(near)

    loads = [
        pltpu.make_async_copy(source, target, load_sem.at[index])
        for index, (source, target) in enumerate(
            (
                (positions_hbm, positions),
                (angles_hbm, angles),
                (areas_hbm, areas),
                (assign_hbm, assign),
                (visible_hbm, visible),
                (b_hbm, b_full),
                (emission_hbm, emission),
                (reflect_hbm, reflect),
            )
        )
    ]
    for load in loads:
        load.start()

    right = (row, (x + 1) % 4 * 4 + col % 4)
    left = (row, (x + 3) % 4 * 4 + col % 4)
    sibling = (row, x * 4 + z_hi * 2 + (1 - core))
    across = (row, x * 4 + (1 - z_hi) * 2 + core)

    barrier = pltpu.get_barrier_semaphore()
    for partner in (right, left, sibling, across):
        pl.semaphore_signal(barrier, inc=1, device_id=partner, device_id_type=MESH)

    @pl.when(near & (x == (home // 4 + 2) % 4))
    def _():
        pl.semaphore_signal(barrier, inc=1, device_id=(row, home), device_id_type=MESH)

    for load in loads[0:4]:
        load.wait()
    table[0:3, :] = positions[...]
    table[3:5, :] = angles[...]
    table[5:6, :] = areas[...]
    table[6:7, :] = assign[...].astype(F32)
    table[7:8, :] = jnp.zeros((1, COLS), F32)
    pl.semaphore_wait(barrier, jnp.where(is_source, 5, 4))

    def spread(hop):
        return pltpu.make_async_remote_copy(
            src_ref=table.at[:, pl.ds(pl.multiple_of(row % 2 * ROWS, ROWS), ROWS)],
            dst_ref=row_table,
            send_sem=spread_send.at[hop - 1],
            recv_sem=spread_recv,
            device_id=(row, (x + hop) % 4 * 4 + col % 4),
            device_id_type=MESH,
        )

    forward = pltpu.make_async_remote_copy(
        src_ref=row_table,
        dst_ref=row_table,
        send_sem=forward_send,
        recv_sem=spread_recv,
        device_id=sibling,
        device_id_type=MESH,
    )

    over = pltpu.make_async_remote_copy(
        src_ref=row_table,
        dst_ref=row_table,
        send_sem=over_send,
        recv_sem=spread_recv,
        device_id=across,
        device_id_type=MESH,
    )

    @pl.when(is_source)
    def _():
        for hop in (2, 1, 3):
            spread(hop).start()
        row_table[...] = table[:, pl.ds(pl.multiple_of(row % 2 * ROWS, ROWS), ROWS)]
        over.start()
        forward.start()

    loads[4].wait()
    shut = ((visible[...].astype(F32) - 1.0) * CLOSED).astype(BF16)

    def column_tables(step, carry):
        lanes = pl.ds(pl.multiple_of(step * WIDE, WIDE), WIDE)
        block = table[:, lanes]
        place, pos, normal = facets(block)
        alpha = block[5:6] * (1 / math.pi)
        weighted = normal * alpha
        offset = -jnp.sum(weighted * pos, axis=0, keepdims=True)
        reach = jnp.sum(pos * pos, axis=0, keepdims=True) + alpha
        p1, p2, p3 = pieces(pos)
        m1, m2, m3 = pieces(weighted)
        t1, t2, t3 = pieces(offset)
        w1, w2, w3 = pieces(reach)
        zero = jnp.zeros_like(block)
        ones = jnp.where(place < 3, 1.0, zero)
        one_of[0:128, lanes] = jnp.concatenate(
            [zero] * 8 + [p1, p2, p3, p1, p2, p1, ones, zero], axis=0
        ).astype(BF16)
        two_of[:, lanes] = jnp.concatenate(
            [m1, m2, m3, m1, m2, m1, stacked(place, t1, t2, t3), zero], axis=0
        ).astype(BF16)
        d1, d2, d3 = -2.0 * p1, -2.0 * p2, -2.0 * p3
        dist_of[:, lanes] = jnp.concatenate(
            [d1, d2, d3, d1, d2, d1, stacked(place, w1, w2, w3, 1.0, 1.0, 1.0), zero],
            axis=0,
        ).astype(BF16)
        ids = block[6:7].astype(jnp.int32)
        block_ids = lax.broadcasted_iota(jnp.int32, (128, WIDE), 0)
        onehot = jnp.where(block_ids == ids, 1.0, 0.0).astype(BF16)
        one_of[128:256, lanes] = jnp.dot(shut, onehot, preferred_element_type=F32).astype(BF16)
        return carry

    lax.fori_loop(0, COLS // WIDE, column_tables, 0)

    @pl.when(is_relay)
    def _():
        spread(1).wait_recv()
        over.start()
        forward.start()

    loads[5].wait()

    def split_radiosity(step, carry):
        rows = pl.ds(pl.multiple_of(step * 256, 256), 256)
        value = b_full[rows, :]
        high = value.astype(BF16)
        b_two[rows, 0:128] = high
        b_two[rows, 128:256] = (value - high.astype(F32)).astype(BF16)
        return carry

    lax.fori_loop(0, COLS // 256, split_radiosity, 0)

    @pl.when(is_far)
    def _():
        over.wait_recv()
        forward.start()

    @pl.when(jnp.logical_not(serves))
    def _():
        forward.wait_recv()


    def row_tables(step, carry):
        lanes = pl.ds(pl.multiple_of(step * 256, 256), 256)
        block = row_table[:, lanes]
        place, pos, normal = facets(block)
        start = -jnp.sum(normal * pos, axis=0, keepdims=True)
        reach = jnp.sum(pos * pos, axis=0, keepdims=True)
        q1, q2, q3 = pieces(pos)
        n1, n2, n3 = pieces(normal)
        s1, s2, s3 = pieces(start)
        r1, r2, r3 = pieces(reach)
        zero = jnp.zeros_like(block)
        groups = [q1, q1, q1, q2, q2, q3, stacked(place, 1.0, 1.0, 1.0, r1, r2, r3), zero]
        groups += [n1, n1, n1, n2, n2, n3, stacked(place, s1, s2, s3), zero]
        lhs[lanes, 0:128] = jnp.concatenate(groups, axis=0).T.astype(BF16)
        ids = block[6:7].astype(jnp.int32)
        block_ids = lax.broadcasted_iota(jnp.int32, (128, 256), 0)
        lhs[lanes, 128:256] = jnp.where(block_ids == ids, 1.0, 0.0).T.astype(BF16)
        return carry

    lax.fori_loop(0, ROWS // 256, row_tables, 0)

    def hop_of(piece):
        between = jnp.where(piece % 2 == 1, (piece + 1) // 2, piece // 2 - 1)
        return jnp.where(piece == 0, 0, jnp.where(piece == 7, 3, between))

    def half_of(piece):
        stays = (piece == 7) | ((piece > 0) & (piece % 2 == 0))
        return jnp.where(stays, z_hi, 1 - z_hi)

    def first_row(piece):
        side = half_of(piece)
        hop = hop_of(piece)
        owner = jnp.where(side == 0, x + 3 - hop, x + 1 + hop) % 4
        return pl.multiple_of(owner * 512 + side * PIECE, PIECE)

    slots = ((one_a, two_a, dist_a), (one_b, two_b, dist_b))

    def geometry(begin, tile, slot):
        rows = pl.ds(begin, PIECE)
        lanes = pl.ds(pl.multiple_of(tile * TILE, TILE), TILE)
        slot[0][...] = jnp.dot(lhs[rows, :], one_of[:, lanes], preferred_element_type=F32)
        slot[1][...] = jnp.dot(lhs[rows, 0:64], two_of[:, lanes], preferred_element_type=F32)
        slot[2][...] = jnp.dot(lhs[rows, 0:64], dist_of[:, lanes], preferred_element_type=F32)

    def view(slot, views):
        for lane in range(0, TILE, 128):
            for line in range(0, PIECE, 16):
                part = (slice(line, line + 16), slice(lane, lane + 128))
                dist = slot[2][part]
                both = jnp.maximum(slot[0][part], 0.0) * jnp.maximum(slot[1][part], 0.0)
                views[part] = both * pl.reciprocal(dist * dist, approx=True)

    def gather(tile, views):
        value = views[...]
        high = value.astype(BF16)
        low = (value - high.astype(F32)).astype(BF16)
        rad = b_two[pl.ds(pl.multiple_of(tile * TILE, TILE), TILE), :]
        total = jnp.dot(high, rad, preferred_element_type=F32)
        total += jnp.dot(low, rad, preferred_element_type=F32)
        acc[...] += total

    def ring(piece):
        return pltpu.make_async_remote_copy(
            src_ref=sent.at[piece],
            dst_ref=came.at[piece],
            send_sem=ring_send.at[piece],
            recv_sem=ring_recv.at[piece],
            device_id=(row, (x + jnp.where(piece % 2 == 0, 1, 3)) % 4 * 4 + col % 4),
            device_id_type=MESH,
        )

    other_rows = pl.ds(pl.multiple_of((1 - core) * 128, 128), 128)
    own_rows = pl.ds(pl.multiple_of(core * 128, 128), 128)

    def core_copy(index, source_ref):
        return pltpu.make_async_remote_copy(
            src_ref=source_ref.at[other_rows],
            dst_ref=core_came.at[index],
            send_sem=core_send.at[index],
            recv_sem=core_recv.at[index],
            device_id=sibling,
            device_id_type=MESH,
        )

    z_copy = pltpu.make_async_remote_copy(
        src_ref=z_sent,
        dst_ref=z_came,
        send_sem=z_send,
        recv_sem=z_recv,
        device_id=across,
        device_id_type=MESH,
    )

    def folded():
        return acc[:, 0:128] + acc[:, 128:256]

    pairs = STEPS // 2
    tiles = PIECES * STEPS
    acc[...] = jnp.zeros_like(acc)

    def geometry_of(index, slot):
        geometry(first_row(index // STEPS), index % STEPS, slot)

    geometry_of(0, slots[0])
    view(slots[0], view_a)
    geometry_of(1, slots[1])

    def visit(index, carry):
        piece = index // pairs
        tile = index % pairs * 2
        after = jnp.minimum(index * 2 + 2, tiles - 2)
        geometry_of(after, slots[0])
        view(slots[1], view_b)
        gather(tile, view_a)
        geometry_of(after + 1, slots[1])
        view(slots[0], view_a)
        gather(tile + 1, view_b)

        @pl.when(tile == STEPS - 2)
        def _():
            hop = hop_of(piece)
            place = hop * 2 + half_of(piece)

            @pl.when(hop == 0)
            def _():
                sent[place] = folded()
                ring(place).start()

            @pl.when((hop == 1) | (hop == 2))
            def _():
                ring(place - 2).wait_recv()
                sent[place] = folded() + came[place - 2]
                ring(place).start()

            @pl.when(piece == 5)
            def _():
                ring(5 - z_hi).wait_recv()
                first_half[...] = folded() + came[5 - z_hi]
                core_copy(0, first_half).start()

            @pl.when(piece < 7)
            def _():
                acc[...] = jnp.zeros_like(acc)

        @pl.when((piece == 6) & (tile == 2))
        def _():
            core_copy(0, first_half).wait_recv()
            z_sent[...] = first_half[own_rows, :] + core_came[0]
            z_copy.start()

        return carry

    lax.fori_loop(0, PIECES * pairs, visit, 0)

    ring(4 + z_hi).wait_recv()
    second_half[...] = folded() + came[4 + z_hi]
    core_copy(1, second_half).start()
    z_copy.wait_recv()
    partial = second_half[own_rows, :] + z_came[...]
    core_copy(1, second_half).wait_recv()
    loads[6].wait()
    loads[7].wait()
    out[...] = emission[...] + reflect[...] * (partial + core_came[1])

    @pl.when(is_source)
    def _():
        for hop in range(1, 4):
            spread(hop).wait_send()

    @pl.when(near)
    def _():
        over.wait_send()

    @pl.when(serves)
    def _():
        forward.wait_send()

    for piece in range(6):
        ring(piece).wait_send()
    core_copy(0, first_half).wait_send()
    core_copy(1, second_half).wait_send()
    z_copy.wait_send()


def on_device(b_old, positions, angles, areas, visible, assign, emission, reflect):
    vmem = pl.BlockSpec(memory_space=pltpu.VMEM)
    return pl.pallas_call(
        kernel,
        out_shape=jax.ShapeDtypeStruct((128, BANDS), F32),
        in_specs=[pl.BlockSpec(memory_space=pl.ANY)] * 8,
        out_specs=vmem,
        scratch_shapes=[
            pltpu.VMEM((3, COLS), F32),
            pltpu.VMEM((2, COLS), F32),
            pltpu.VMEM((1, COLS), F32),
            pltpu.VMEM((1, COLS), jnp.int32),
            pltpu.VMEM((8, COLS), F32),
            pltpu.VMEM((COLS, BANDS), F32),
            pltpu.VMEM((128, 128), jnp.int32),
            pltpu.VMEM((128, BANDS), F32),
            pltpu.VMEM((128, BANDS), F32),
            pltpu.VMEM((COLS, 2 * BANDS), BF16),
            pltpu.VMEM((256, COLS), BF16),
            pltpu.VMEM((64, COLS), BF16),
            pltpu.VMEM((64, COLS), BF16),
            pltpu.VMEM((ROWS, 256), BF16),
            pltpu.VMEM((8, ROWS), F32),
            pltpu.VMEM((PIECE, 2 * BANDS), F32),
        ]
        + [pltpu.VMEM((PIECE, TILE), F32)] * 8
        + [
            pltpu.VMEM((6, PIECE, BANDS), F32),
            pltpu.VMEM((6, PIECE, BANDS), F32),
            pltpu.VMEM((PIECE, BANDS), F32),
            pltpu.VMEM((PIECE, BANDS), F32),
            pltpu.VMEM((2, 128, BANDS), F32),
            pltpu.VMEM((128, BANDS), F32),
            pltpu.VMEM((128, BANDS), F32),
            pltpu.SemaphoreType.DMA((8,)),
            pltpu.SemaphoreType.DMA((3,)),
            pltpu.SemaphoreType.DMA,
            pltpu.SemaphoreType.DMA,
            pltpu.SemaphoreType.DMA,
            pltpu.SemaphoreType.DMA((6,)),
            pltpu.SemaphoreType.DMA((6,)),
            pltpu.SemaphoreType.DMA((2,)),
            pltpu.SemaphoreType.DMA((2,)),
            pltpu.SemaphoreType.DMA,
            pltpu.SemaphoreType.DMA,
        ],
        compiler_params=pltpu.CompilerParams(
            collective_id=0, has_side_effects=True, vmem_limit_bytes=60 * 2**20
        ),
        name="radiosity",
    )(
        positions,
        angles,
        areas[None, :],
        assign[None, :],
        b_old,
        visible,
        emission,
        reflect,
    )


def solution(mesh):
    return jax.shard_map(
        on_device,
        mesh=mesh,
        in_specs=(
            P("col", None),
            P(None, "col"),
            P(None, "col"),
            P("col"),
            P(),
            P("col"),
            P(("row", "col"), None),
            P(("row", "col"), None),
        ),
        out_specs=P(("row", "col"), None),
        check_vma=False,
    )
```

```python
import math

import jax
import jax.numpy as jnp
from jax import lax
from jax.experimental import pallas as pl
from jax.experimental.pallas import tpu as pltpu
from jax.sharding import PartitionSpec as P

F32 = jnp.float32
BF16 = jnp.bfloat16
MESH = pl.DeviceIdType.MESH

ROWS = 2048
COLS = 4096
BANDS = 128
PIECE = 256
TILE = 1024
STEPS = COLS // TILE
PIECES = ROWS // PIECE
PARTS = 4
PART = ROWS // PARTS
WIDE = 512
CLOSED = 64.0

SIN = (-1 / 6, 1 / 120, -1 / 5040, 1 / 362880, -1 / 39916800, 1 / 6227020800)
COS = (-1 / 2, 1 / 24, -1 / 720, 1 / 40320, -1 / 3628800, 1 / 479001600, -1 / 87178291200)


def sin_cos(angle):
    turns = jnp.floor(angle * (1 / math.pi) + 0.5)
    rest = (angle - turns * 3.140625) - turns * (math.pi - 3.140625)
    sign = 1.0 - 2.0 * (turns * turns)
    square = rest * rest
    odd = jnp.full_like(angle, SIN[-1])
    for factor in SIN[-2::-1]:
        odd = odd * square + factor
    even = jnp.full_like(angle, COS[-1])
    for factor in COS[-2::-1]:
        even = even * square + factor
    return sign * (rest + rest * (square * odd)), sign * (1.0 + square * even)


def rounded(x):
    return x.astype(BF16).astype(F32)


def pieces(x):
    first = rounded(x)
    rest = x - first
    second = rounded(rest)
    return first, second, rounded(rest - second)


def facets(block):
    place = lax.broadcasted_iota(jnp.int32, block.shape, 0)
    pos = jnp.where(place < 3, block, 0.0)
    sine, cosine = sin_cos(block)
    flat = cosine[4:5]
    normal = jnp.where(
        place == 0,
        cosine[3:4] * flat,
        jnp.where(place == 1, sine[3:4] * flat, jnp.where(place == 2, sine[4:5], 0.0)),
    )
    return place, pos, normal


def stacked(place, *lines):
    out = jnp.zeros(place.shape, F32)
    for index, line in enumerate(lines):
        out = jnp.where(place == index, line, out)
    return out


def kernel(
    positions_hbm,
    angles_hbm,
    areas_hbm,
    assign_hbm,
    b_hbm,
    visible_hbm,
    emission_hbm,
    reflect_hbm,
    out,
    positions,
    angles,
    areas,
    assign,
    table,
    b_full,
    visible,
    emission,
    reflect,
    b_two,
    one_of,
    two_of,
    dist_of,
    lhs,
    row_table,
    acc,
    one_a,
    two_a,
    dist_a,
    one_b,
    two_b,
    dist_b,
    view_a,
    view_b,
    sent,
    came,
    first_half,
    second_half,
    core_came,
    z_sent,
    z_came,
    load_sem,
    spread_send,
    over_send,
    forward_send,
    spread_recv,
    ring_send,
    ring_recv,
    core_send,
    core_recv,
    z_send,
    z_recv,
):
    row = lax.axis_index("row")
    col = lax.axis_index("col")
    x = col // 4
    z_hi = col // 2 % 2
    core = col % 2
    home = row // 2
    serves = core == home % 2
    near = serves & (z_hi == home // 2 % 2)
    is_source = col == home
    is_relay = near & jnp.logical_not(is_source)
    is_far = serves & jnp.logical_not(near)

    loads = [
        pltpu.make_async_copy(source, target, load_sem.at[index])
        for index, (source, target) in enumerate(
            (
                (positions_hbm, positions),
                (angles_hbm, angles),
                (areas_hbm, areas),
                (assign_hbm, assign),
                (visible_hbm, visible),
                (b_hbm, b_full),
                (emission_hbm, emission),
                (reflect_hbm, reflect),
            )
        )
    ]
    for load in loads:
        load.start()

    right = (row, (x + 1) % 4 * 4 + col % 4)
    left = (row, (x + 3) % 4 * 4 + col % 4)
    sibling = (row, x * 4 + z_hi * 2 + (1 - core))
    across = (row, x * 4 + (1 - z_hi) * 2 + core)

    barrier = pltpu.get_barrier_semaphore()
    for partner in (right, left, sibling, across):
        pl.semaphore_signal(barrier, inc=1, device_id=partner, device_id_type=MESH)

    @pl.when(near & (x == (home // 4 + 2) % 4))
    def _():
        pl.semaphore_signal(barrier, inc=1, device_id=(row, home), device_id_type=MESH)

    for load in loads[0:4]:
        load.wait()
    table[0:3, :] = positions[...]
    table[3:5, :] = angles[...]
    table[5:6, :] = areas[...]
    table[6:7, :] = assign[...].astype(F32)
    table[7:8, :] = jnp.zeros((1, COLS), F32)
    pl.semaphore_wait(barrier, jnp.where(is_source, 5, 4))

    def lanes_of(part):
        return pl.ds(part * PART, PART)

    def spread(hop, part):
        return pltpu.make_async_remote_copy(
            src_ref=table.at[:, pl.ds(pl.multiple_of(row % 2 * ROWS + part * PART, PART), PART)],
            dst_ref=row_table.at[:, lanes_of(part)],
            send_sem=spread_send.at[(hop - 1) * PARTS + part],
            recv_sem=spread_recv.at[part],
            device_id=(row, (x + hop) % 4 * 4 + col % 4),
            device_id_type=MESH,
        )

    def forward(part):
        return pltpu.make_async_remote_copy(
            src_ref=row_table.at[:, lanes_of(part)],
            dst_ref=row_table.at[:, lanes_of(part)],
            send_sem=forward_send.at[part],
            recv_sem=spread_recv.at[part],
            device_id=sibling,
            device_id_type=MESH,
        )

    def over(part):
        return pltpu.make_async_remote_copy(
            src_ref=row_table.at[:, lanes_of(part)],
            dst_ref=row_table.at[:, lanes_of(part)],
            send_sem=over_send.at[part],
            recv_sem=spread_recv.at[part],
            device_id=across,
            device_id_type=MESH,
        )

    @pl.when(is_source)
    def _():
        for part in range(PARTS):
            for hop in (2, 1, 3):
                spread(hop, part).start()
        row_table[...] = table[:, pl.ds(pl.multiple_of(row % 2 * ROWS, ROWS), ROWS)]
        for part in range(PARTS):
            over(part).start()
            forward(part).start()

    loads[4].wait()
    shut = ((visible[...].astype(F32) - 1.0) * CLOSED).astype(BF16)

    def column_tables(step, carry):
        lanes = pl.ds(pl.multiple_of(step * WIDE, WIDE), WIDE)
        block = table[:, lanes]
        place, pos, normal = facets(block)
        alpha = block[5:6] * (1 / math.pi)
        weighted = normal * alpha
        offset = -jnp.sum(weighted * pos, axis=0, keepdims=True)
        reach = jnp.sum(pos * pos, axis=0, keepdims=True) + alpha
        p1, p2, p3 = pieces(pos)
        m1, m2, m3 = pieces(weighted)
        t1, t2, t3 = pieces(offset)
        w1, w2, w3 = pieces(reach)
        zero = jnp.zeros_like(block)
        ones = jnp.where(place < 3, 1.0, zero)
        one_of[0:128, lanes] = jnp.concatenate(
            [zero] * 8 + [p1, p2, p3, p1, p2, p1, ones, zero], axis=0
        ).astype(BF16)
        two_of[:, lanes] = jnp.concatenate(
            [m1, m2, m3, m1, m2, m1, stacked(place, t1, t2, t3), zero], axis=0
        ).astype(BF16)
        d1, d2, d3 = -2.0 * p1, -2.0 * p2, -2.0 * p3
        dist_of[:, lanes] = jnp.concatenate(
            [d1, d2, d3, d1, d2, d1, stacked(place, w1, w2, w3, 1.0, 1.0, 1.0), zero],
            axis=0,
        ).astype(BF16)
        ids = block[6:7].astype(jnp.int32)
        block_ids = lax.broadcasted_iota(jnp.int32, (128, WIDE), 0)
        onehot = jnp.where(block_ids == ids, 1.0, 0.0).astype(BF16)
        one_of[128:256, lanes] = jnp.dot(shut, onehot, preferred_element_type=F32).astype(BF16)
        return carry

    lax.fori_loop(0, COLS // WIDE, column_tables, 0)

    @pl.when(is_relay)
    def _():
        for part in range(PARTS):
            spread(1, part).wait_recv()
            over(part).start()
            forward(part).start()

    loads[5].wait()

    def split_radiosity(step, carry):
        rows = pl.ds(pl.multiple_of(step * 256, 256), 256)
        value = b_full[rows, :]
        high = value.astype(BF16)
        b_two[rows, 0:128] = high
        b_two[rows, 128:256] = (value - high.astype(F32)).astype(BF16)
        return carry

    lax.fori_loop(0, COLS // 256, split_radiosity, 0)

    @pl.when(is_far)
    def _():
        for part in range(PARTS):
            over(part).wait_recv()
            forward(part).start()

    @pl.when(jnp.logical_not(serves))
    def _():
        forward(0).wait_recv()


    def row_tables(step, carry):
        lanes = pl.ds(pl.multiple_of(step * 256, 256), 256)
        block = row_table[:, lanes]
        place, pos, normal = facets(block)
        start = -jnp.sum(normal * pos, axis=0, keepdims=True)
        reach = jnp.sum(pos * pos, axis=0, keepdims=True)
        q1, q2, q3 = pieces(pos)
        n1, n2, n3 = pieces(normal)
        s1, s2, s3 = pieces(start)
        r1, r2, r3 = pieces(reach)
        zero = jnp.zeros_like(block)
        groups = [q1, q1, q1, q2, q2, q3, stacked(place, 1.0, 1.0, 1.0, r1, r2, r3), zero]
        groups += [n1, n1, n1, n2, n2, n3, stacked(place, s1, s2, s3), zero]
        lhs[lanes, 0:128] = jnp.concatenate(groups, axis=0).T.astype(BF16)
        ids = block[6:7].astype(jnp.int32)
        block_ids = lax.broadcasted_iota(jnp.int32, (128, 256), 0)
        lhs[lanes, 128:256] = jnp.where(block_ids == ids, 1.0, 0.0).T.astype(BF16)
        return carry

    per_part = PART // 256
    lax.fori_loop(0, per_part, row_tables, 0)
    for part in range(1, PARTS):

        @pl.when(jnp.logical_not(serves))
        def _(part=part):
            forward(part).wait_recv()

        lax.fori_loop(part * per_part, (part + 1) * per_part, row_tables, 0)

    def hop_of(piece):
        between = jnp.where(piece % 2 == 1, (piece + 1) // 2, piece // 2 - 1)
        return jnp.where(piece == 0, 0, jnp.where(piece == 7, 3, between))

    def half_of(piece):
        stays = (piece == 7) | ((piece > 0) & (piece % 2 == 0))
        return jnp.where(stays, z_hi, 1 - z_hi)

    def first_row(piece):
        side = half_of(piece)
        hop = hop_of(piece)
        owner = jnp.where(side == 0, x + 3 - hop, x + 1 + hop) % 4
        return pl.multiple_of(owner * 512 + side * PIECE, PIECE)

    slots = ((one_a, two_a, dist_a), (one_b, two_b, dist_b))

    def geometry(begin, tile, slot):
        rows = pl.ds(begin, PIECE)
        lanes = pl.ds(pl.multiple_of(tile * TILE, TILE), TILE)
        slot[0][...] = jnp.dot(lhs[rows, :], one_of[:, lanes], preferred_element_type=F32)
        slot[1][...] = jnp.dot(lhs[rows, 0:64], two_of[:, lanes], preferred_element_type=F32)
        slot[2][...] = jnp.dot(lhs[rows, 0:64], dist_of[:, lanes], preferred_element_type=F32)

    def view(slot, views):
        for lane in range(0, TILE, 128):
            for line in range(0, PIECE, 16):
                part = (slice(line, line + 16), slice(lane, lane + 128))
                dist = slot[2][part]
                both = jnp.maximum(slot[0][part], 0.0) * jnp.maximum(slot[1][part], 0.0)
                views[part] = both * pl.reciprocal(dist * dist, approx=True)

    def gather(tile, views):
        value = views[...]
        high = value.astype(BF16)
        low = (value - high.astype(F32)).astype(BF16)
        rad = b_two[pl.ds(pl.multiple_of(tile * TILE, TILE), TILE), :]
        total = jnp.dot(high, rad, preferred_element_type=F32)
        total += jnp.dot(low, rad, preferred_element_type=F32)
        acc[...] += total

    def ring(piece):
        return pltpu.make_async_remote_copy(
            src_ref=sent.at[piece],
            dst_ref=came.at[piece],
            send_sem=ring_send.at[piece],
            recv_sem=ring_recv.at[piece],
            device_id=(row, (x + jnp.where(piece % 2 == 0, 1, 3)) % 4 * 4 + col % 4),
            device_id_type=MESH,
        )

    other_rows = pl.ds(pl.multiple_of((1 - core) * 128, 128), 128)
    own_rows = pl.ds(pl.multiple_of(core * 128, 128), 128)

    def core_copy(index, source_ref):
        return pltpu.make_async_remote_copy(
            src_ref=source_ref.at[other_rows],
            dst_ref=core_came.at[index],
            send_sem=core_send.at[index],
            recv_sem=core_recv.at[index],
            device_id=sibling,
            device_id_type=MESH,
        )

    z_copy = pltpu.make_async_remote_copy(
        src_ref=z_sent,
        dst_ref=z_came,
        send_sem=z_send,
        recv_sem=z_recv,
        device_id=across,
        device_id_type=MESH,
    )

    def folded():
        return acc[:, 0:128] + acc[:, 128:256]

    pairs = STEPS // 2
    tiles = PIECES * STEPS
    acc[...] = jnp.zeros_like(acc)

    def geometry_of(index, slot):
        geometry(first_row(index // STEPS), index % STEPS, slot)

    geometry_of(0, slots[0])
    view(slots[0], view_a)
    geometry_of(1, slots[1])

    def visit(index, carry):
        piece = index // pairs
        tile = index % pairs * 2
        after = jnp.minimum(index * 2 + 2, tiles - 2)
        geometry_of(after, slots[0])
        view(slots[1], view_b)
        gather(tile, view_a)
        geometry_of(after + 1, slots[1])
        view(slots[0], view_a)
        gather(tile + 1, view_b)

        @pl.when(tile == STEPS - 2)
        def _():
            hop = hop_of(piece)
            place = hop * 2 + half_of(piece)

            @pl.when(hop == 0)
            def _():
                sent[place] = folded()
                ring(place).start()

            @pl.when((hop == 1) | (hop == 2))
            def _():
                ring(place - 2).wait_recv()
                sent[place] = folded() + came[place - 2]
                ring(place).start()

            @pl.when(piece == 5)
            def _():
                ring(5 - z_hi).wait_recv()
                first_half[...] = folded() + came[5 - z_hi]
                core_copy(0, first_half).start()

            @pl.when(piece < 7)
            def _():
                acc[...] = jnp.zeros_like(acc)

        @pl.when((piece == 6) & (tile == 0))
        def _():
            core_copy(0, first_half).wait_recv()
            z_sent[...] = first_half[own_rows, :] + core_came[0]
            z_copy.start()

        return carry

    lax.fori_loop(0, PIECES * pairs, visit, 0)

    ring(4 + z_hi).wait_recv()
    second_half[...] = folded() + came[4 + z_hi]
    core_copy(1, second_half).start()
    z_copy.wait_recv()
    partial = second_half[own_rows, :] + z_came[...]
    core_copy(1, second_half).wait_recv()
    loads[6].wait()
    loads[7].wait()
    out[...] = emission[...] + reflect[...] * (partial + core_came[1])

    @pl.when(is_source)
    def _():
        for hop in range(1, 4):
            for part in range(PARTS):
                spread(hop, part).wait_send()

    @pl.when(near)
    def _():
        for part in range(PARTS):
            over(part).wait_send()

    @pl.when(serves)
    def _():
        for part in range(PARTS):
            forward(part).wait_send()

    for piece in range(6):
        ring(piece).wait_send()
    core_copy(0, first_half).wait_send()
    core_copy(1, second_half).wait_send()
    z_copy.wait_send()


def on_device(b_old, positions, angles, areas, visible, assign, emission, reflect):
    vmem = pl.BlockSpec(memory_space=pltpu.VMEM)
    return pl.pallas_call(
        kernel,
        out_shape=jax.ShapeDtypeStruct((128, BANDS), F32),
        in_specs=[pl.BlockSpec(memory_space=pl.ANY)] * 8,
        out_specs=vmem,
        scratch_shapes=[
            pltpu.VMEM((3, COLS), F32),
            pltpu.VMEM((2, COLS), F32),
            pltpu.VMEM((1, COLS), F32),
            pltpu.VMEM((1, COLS), jnp.int32),
            pltpu.VMEM((8, COLS), F32),
            pltpu.VMEM((COLS, BANDS), F32),
            pltpu.VMEM((128, 128), jnp.int32),
            pltpu.VMEM((128, BANDS), F32),
            pltpu.VMEM((128, BANDS), F32),
            pltpu.VMEM((COLS, 2 * BANDS), BF16),
            pltpu.VMEM((256, COLS), BF16),
            pltpu.VMEM((64, COLS), BF16),
            pltpu.VMEM((64, COLS), BF16),
            pltpu.VMEM((ROWS, 256), BF16),
            pltpu.VMEM((8, ROWS), F32),
            pltpu.VMEM((PIECE, 2 * BANDS), F32),
        ]
        + [pltpu.VMEM((PIECE, TILE), F32)] * 8
        + [
            pltpu.VMEM((6, PIECE, BANDS), F32),
            pltpu.VMEM((6, PIECE, BANDS), F32),
            pltpu.VMEM((PIECE, BANDS), F32),
            pltpu.VMEM((PIECE, BANDS), F32),
            pltpu.VMEM((2, 128, BANDS), F32),
            pltpu.VMEM((128, BANDS), F32),
            pltpu.VMEM((128, BANDS), F32),
            pltpu.SemaphoreType.DMA((8,)),
            pltpu.SemaphoreType.DMA((3 * PARTS,)),
            pltpu.SemaphoreType.DMA((PARTS,)),
            pltpu.SemaphoreType.DMA((PARTS,)),
            pltpu.SemaphoreType.DMA((PARTS,)),
            pltpu.SemaphoreType.DMA((6,)),
            pltpu.SemaphoreType.DMA((6,)),
            pltpu.SemaphoreType.DMA((2,)),
            pltpu.SemaphoreType.DMA((2,)),
            pltpu.SemaphoreType.DMA,
            pltpu.SemaphoreType.DMA,
        ],
        compiler_params=pltpu.CompilerParams(
            collective_id=0, has_side_effects=True, vmem_limit_bytes=60 * 2**20
        ),
        name="radiosity",
    )(
        positions,
        angles,
        areas[None, :],
        assign[None, :],
        b_old,
        visible,
        emission,
        reflect,
    )


def solution(mesh):
    return jax.shard_map(
        on_device,
        mesh=mesh,
        in_specs=(
            P("col", None),
            P(None, "col"),
            P(None, "col"),
            P("col"),
            P(),
            P("col"),
            P(("row", "col"), None),
            P(("row", "col"), None),
        ),
        out_specs=P(("row", "col"), None),
        check_vma=False,
    )
```
